256 devices in a mesh: freq: 32 (over z_hi, x, core), src: 8 (over z_lo, y).
Axes of the slice: x: 4, y: 4, z: 8 (z_hi: 4, z_lo: 2; z = z_hi * 2 + z_lo), core: 2. Of those that a mesh axis runs over, the one named last changes fastest.
Arguments:
- reflection: float32 [2, 256, 1024, 1024], P(None, 'freq', 'src'), as said below
- focusing: float32 [2, 256, 64, 1024], P(None, 'freq', None, 'src'), may hold values from -6 to 6
- onsets: int32 [64, 1024], P('freq', 'src'), may hold values from 1 to 128
Outputs:
- downgoing: float32 [2, 256, 64, 1024], P(None, 'freq', None, 'src')
- upgoing: float32 [2, 256, 64, 1024], P(None, 'freq', None, 'src')
The draws below stay inside these ranges and needn't reach their ends.
Inputs may be any that keep to these rules, and one draw needn't show every extreme that they name: reflection[c, f, s, r] equals reflection[c, f, r, s] (reciprocity).
All inputs are finite; a program needn't handle non-finite values.
Results may differ from the reference program's by a relative error of at most 0.00014.
Values sent between devices are 32-bit elements; how exact they have to be, the bound alone decides.
A program may use at most 64 MiB of HBM per device.

```python
import math
import jax
import jax.numpy as jnp
from jax import lax

N = 1024
NF = 256
P_SIZE = 64
ITERS = 2


def draw_reflection(key, part):
    key = jax.random.fold_in(key, 11)
    first_key = jax.random.fold_in(key, 0)
    shape = (2, NF, N, N)
    sample_values = jax.random.normal(first_key, shape, jnp.float32)
    symmetric = (sample_values + jnp.swapaxes(sample_values, 2, 3)) * (0.4 * 0.70710678 / math.sqrt(N))
    return symmetric.astype(jnp.float32)


def touch_ends(drawn, own_key, smallest, high):
    longest = drawn.shape.index(max(drawn.shape))
    spots = []
    for shift in (0, 1):
        where = [jax.random.randint(jax.random.fold_in(own_key, axis), (), 0, length) for axis, length in enumerate(drawn.shape)]
        where[longest] = (where[longest] + shift) % drawn.shape[longest]
        spots.append(tuple(where))
    return drawn.at[spots[0]].set(smallest).at[spots[1]].set(high)


def shard_levels(key, extent, cuts, smallest, largest):
    def one(axis_at, parts):
        heights = jax.random.uniform(jax.random.fold_in(jax.random.fold_in(key, 6), axis_at), (parts,), jnp.float32, smallest / len(cuts), largest / len(cuts))
        return jnp.repeat(jnp.exp(heights), extent[axis_at] // parts).reshape((-1,) + (1,) * (len(extent) - axis_at - 1))

    level = one(*cuts[0])
    for cut in cuts[1:]:
        level = level * one(*cut)
    return level


def noise(key, dims, scale, reach, cuts=(), kind=jnp.bfloat16):
    factor_of = shard_levels(key, dims, cuts, -0.22, 0.18) if cuts else 1.0
    array = jax.random.normal(key, dims, jnp.float32) * scale * factor_of
    return jnp.minimum(jnp.maximum(array, -reach), reach).astype(kind)


def setup_inputs(seed: int = 0) -> dict:
    arg_keys = jax.random.split(jax.random.key(seed), 4)
    return {
        "reflection": draw_reflection(jax.random.fold_in(arg_keys[3], 71), 0),
        "focusing": noise(arg_keys[1], (2, NF, P_SIZE, N), 1.0, 6.0, ((1, 32), (3, 8)), jnp.float32),
        "onsets": touch_ends(jax.random.randint(arg_keys[2], (P_SIZE, N), 1, NF // 2 + 1), jax.random.fold_in(arg_keys[2], 1), 1, (NF // 2 + 1) - 1).astype(jnp.int32),
    }


def dft_tables(length):
    samples = jnp.arange(length, dtype=jnp.int32)
    phases = (samples[:, None] * samples[None, :]) % length
    phase_angles = phases.astype(jnp.float32) * (2.0 * math.pi / length)
    return jnp.cos(phase_angles), jnp.sin(phase_angles)


def transform(table, sample_values):
    return jnp.einsum("tf,fpx->tpx", table, sample_values, precision=lax.Precision.HIGHEST)


def window_traces(spectra, onsets):
    length = spectra.shape[1]
    cosine_lookup, sin_table = dft_tables(length)
    real_part, imag_part = spectra[0], spectra[1]
    time_real = (transform(cosine_lookup, real_part) - transform(sin_table, imag_part)) / length
    time_imag = (transform(sin_table, real_part) + transform(cosine_lookup, imag_part)) / length
    samples = jnp.arange(length, dtype=jnp.int32)
    nearest = jnp.minimum(samples, length - samples)
    kept_mask = (nearest[:, None, None] < onsets[None]).astype(time_real.dtype)
    time_real = time_real * kept_mask
    time_imag = time_imag * kept_mask
    back_real = transform(cosine_lookup, time_real) + transform(sin_table, time_imag)
    back_imag = transform(cosine_lookup, time_imag) - transform(sin_table, time_real)
    return jnp.stack([back_real, back_imag])


def product(layout_kind, left, right):
    return jnp.einsum(layout_kind, left, right, precision=lax.Precision.HIGHEST)


def reference(reflection, focusing, onsets):
    refl_real, refl_imag = reflection[0], reflection[1]
    downgoing = focusing
    upgoing = focusing
    for iteration in range(ITERS):
        layout_kind = "idt,iqt->iqd"
        forward_real = product(layout_kind, refl_real, downgoing[0]) - product(layout_kind, refl_imag, downgoing[1])
        forward_imag = product(layout_kind, refl_real, downgoing[1]) + product(layout_kind, refl_imag, downgoing[0])
        upgoing = window_traces(jnp.stack([forward_real, forward_imag]), onsets)
        layout_kind = "jkn,juk->jun"
        adjoint_real = product(layout_kind, refl_real, upgoing[0]) + product(layout_kind, refl_imag, upgoing[1])
        transposed_imaginary = product(layout_kind, refl_real, upgoing[1]) - product(layout_kind, refl_imag, upgoing[0])
        downgoing = focusing - window_traces(jnp.stack([adjoint_real, transposed_imaginary]), onsets)
    return downgoing, upgoing
```

```python
import math

import jax
import jax.numpy as jnp
import ml_dtypes
import numpy as np
from jax import lax
from jax.experimental import pallas as pl
from jax.experimental.pallas import tpu as pltpu
from jax.sharding import PartitionSpec as P

ITERS = 2
NFD = 32
NSD = 8
NY = 4
FL = 8
NC = 2
NQ = 32
MSG = 2 * FL
ROWS = NQ * MSG
HALF = ROWS // 2
LANES = 128
NF = 256
MESH = pl.DeviceIdType.MESH
F32 = jnp.float32
BF16 = jnp.bfloat16


def tables():
    samples = np.arange(NF)
    angles = (samples[:, None] * samples[None, :] % NF) * (2.0 * math.pi / NF)
    table = np.concatenate([np.cos(angles), np.sin(angles)], 0).astype(np.float32)
    high = table.astype(ml_dtypes.bfloat16)
    low = (table - high.astype(np.float32)).astype(ml_dtypes.bfloat16)
    return high, low


def split(values):
    high = values.astype(BF16)
    return high, (values - high.astype(F32)).astype(BF16)


def dot(left, right):
    return jnp.dot(left, right, preferred_element_type=F32)


def dot_t(left, right):
    return lax.dot_general(left, right, (((1,), (1,)), ((), ())), preferred_element_type=F32)


def kernel(
    refl, foc, onsets, th, tl, down_out, up_out,
    rstage, rhi, rlo, ag, part, r1, r2, rz, sbuf, rbuf,
    stage_sem, a2a_send, a2a_recv, ag_send, ag_recv, rs_send, rs_recv,
):
    me = lax.axis_index("freq")
    src = lax.axis_index("src")
    z = src // NY
    y = lax.rem(src, NY)
    z1 = 1 - z
    yp = lax.rem(y + 1, NY)
    ym = lax.rem(y + NY - 1, NY)
    y2 = lax.rem(y + 2, NY)
    dev_p = (me, z * NY + yp)
    dev_m = (me, z * NY + ym)
    dev_z = (me, z1 * NY + y)
    pending = []

    barrier = pltpu.get_barrier_semaphore()
    for dev in (dev_p, dev_m, dev_z):
        pl.semaphore_signal(barrier, inc=1, device_id=dev, device_id_type=MESH)

    def greet(k, carry):
        pl.semaphore_signal(
            barrier, inc=1, device_id=(lax.rem(me + k, NFD), src), device_id_type=MESH
        )
        return carry

    lax.fori_loop(1, NFD, greet, 0)

    def stage_copy(f):
        return pltpu.make_async_copy(refl.at[:, f], rstage.at[f % 2], stage_sem.at[f % 2])

    stage_copy(0).start()
    stage_copy(1).start()

    def lay_out(h):
        for c in range(2):
            for f in range(FL):
                ag[0, h, src, pl.ds(c * FL + f, NQ, stride=MSG), :] = foc[
                    c, f, pl.ds(h, NQ, stride=NC), :
                ]

    def prepare(f):
        stage_copy(f).wait()
        for c in range(2):
            high, low = split(rstage[f % 2, c])
            rhi[f, c * LANES : (c + 1) * LANES, :] = high
            rlo[f, c * LANES : (c + 1) * LANES, :] = low
        if f + 2 < FL:
            stage_copy(f + 2).start()

    def rows_of(half):
        return pl.ds(half * HALF, HALF)

    def remote(source, target, send_sem, recv_sem, dev):
        copy = pltpu.make_async_remote_copy(
            source, target, send_sem, recv_sem, device_id=dev, device_id_type=MESH
        )
        copy.start()
        pending.append(copy)

    def landed(target, sem):
        pltpu.make_async_copy(target, target, sem).wait()

    def ag_msg(it, h, slot, half, number, dev):
        piece = ag.at[it, h, slot, rows_of(half)]
        remote(piece, piece, ag_send.at[it, h, number], ag_recv.at[it, h, number], dev)

    def ag_landed(it, h, slot, half, number):
        landed(ag.at[it, h, slot, rows_of(half)], ag_recv.at[it, h, number])

    def ag_start(it, h):
        for half in range(2):
            ag_msg(it, h, src, half, half, dev_z)
            ag_msg(it, h, src, half, 2 + half, dev_p)
            ag_msg(it, h, src, 1 - half, 4 + 1 - half, dev_m)

    def ag_forward_z(it, h):
        other = z1 * NY + y
        for half in range(2):
            ag_landed(it, h, other, half, half)
            ag_msg(it, h, other, half, 6 + half, dev_p)
            ag_msg(it, h, other, half, 8 + half, dev_m)

    def ag_forward_y(it, h):
        for row, base, number in ((z, 2, 10), (z1, 6, 12)):
            ag_landed(it, h, row * NY + ym, 0, base)
            ag_msg(it, h, row * NY + ym, 0, number, dev_p)
            ag_landed(it, h, row * NY + yp, 1, base + 3)
            ag_msg(it, h, row * NY + yp, 1, number + 1, dev_m)

    def ag_finish(it, h):
        for row, base, number in ((z, 2, 10), (z1, 6, 12)):
            ag_landed(it, h, row * NY + ym, 1, base + 1)
            ag_landed(it, h, row * NY + yp, 0, base + 2)
            ag_landed(it, h, row * NY + y2, 0, number)
            ag_landed(it, h, row * NY + y2, 1, number + 1)

    def a2a_start(it, h, k):
        def send(step, carry):
            peer = lax.rem(me + step, NFD)
            pltpu.make_async_remote_copy(
                sbuf.at[it, h, k, pl.ds(pl.multiple_of(peer * MSG, MSG), MSG)],
                rbuf.at[it, h, k, pl.ds(pl.multiple_of(me * MSG, MSG), MSG)],
                a2a_send.at[it, h, k],
                a2a_recv.at[it, h, k],
                device_id=(peer, src),
                device_id_type=MESH,
            ).start()
            return carry

        lax.fori_loop(1, NFD, send, 0)
        own = pl.ds(pl.multiple_of(me * MSG, MSG), MSG)
        rbuf[it, h, k, own, :] = sbuf[it, h, k, own, :]

    def a2a_wait(it, h, k):
        landed(rbuf.at[it, h, k, pl.ds(0, ROWS - MSG)], a2a_recv.at[it, h, k])

    def a2a_sent(it, h, k):
        landed(sbuf.at[it, h, k, pl.ds(0, ROWS - MSG)], a2a_send.at[it, h, k])

    def forward(it, h):
        def one(f, carry):
            real = [ag[it, h, s, pl.ds(f, NQ, stride=MSG), :] for s in range(NSD)]
            imag = [ag[it, h, s, pl.ds(FL + f, NQ, stride=MSG), :] for s in range(NSD)]
            field = jnp.concatenate(
                [jnp.concatenate(real, axis=1), jnp.concatenate(imag, axis=1)], axis=0
            )
            high, low = split(field)
            both = dot_t(jnp.concatenate([high, low], axis=0), rhi[f])
            total = both[: 2 * NQ] + both[2 * NQ :] + dot_t(high, rlo[f])
            sbuf[it, h, 0, pl.ds(f, NQ, stride=MSG), :] = (
                total[:NQ, :LANES] - total[NQ:, LANES:]
            )
            sbuf[it, h, 0, pl.ds(FL + f, NQ, stride=MSG), :] = (
                total[:NQ, LANES:] + total[NQ:, :LANES]
            )
            return carry

        lax.fori_loop(0, FL, one, 0)
        a2a_start(it, h, 0)

    def transform(values):
        high, low = split(values)
        return dot(th[...], high) + (dot(tl[...], high) + dot(th[...], low))

    def window(it, h, k):
        a2a_wait(it, h, k)
        received = rbuf[it, h, k].reshape(NFD, 2, FL, LANES)
        spectra = jnp.concatenate(
            [received[:, 0].reshape(NF, LANES), received[:, 1].reshape(NF, LANES)], axis=1
        )
        times = transform(spectra)
        sample = lax.broadcasted_iota(jnp.int32, (NF, LANES), 0)
        nearest = jnp.minimum(sample, NF - sample)
        kept = jnp.where(nearest < onsets[h : h + 1, :], 1.0 / NF, 0.0).astype(F32)
        real = (times[:NF, :LANES] - times[NF:, LANES:]) * kept
        imag = (times[NF:, :LANES] + times[:NF, LANES:]) * kept
        back = transform(jnp.concatenate([real, imag], axis=1))
        back_real = back[:NF, :LANES] + back[NF:, LANES:]
        back_imag = back[:NF, LANES:] - back[NF:, :LANES]
        sbuf[it, h, k + 1] = jnp.concatenate(
            [back_real.reshape(NFD, 1, FL, LANES), back_imag.reshape(NFD, 1, FL, LANES)], axis=1
        ).reshape(ROWS, LANES)
        a2a_start(it, h, k + 1)

    def rs_msg(source, target, it, h, number, dev):
        remote(source, target, rs_send.at[it, h, number], rs_recv.at[it, h, number], dev)

    def rs_second(it, h, row, direction, half):
        column, dev = ((yp, dev_p), (ym, dev_m))[direction]
        rs_msg(
            part.at[it, h, row * NY + column, rows_of(half)],
            r2.at[it, h, row * 2 + direction, rows_of(half)],
            it, h, 4 + row * 4 + direction * 2 + half, dev,
        )

    def adjoint(it, h):
        a2a_wait(it, h, 1)

        def one(f, carry):
            real = rbuf[it, h, 1, pl.ds(f, NQ, stride=MSG), :]
            imag = rbuf[it, h, 1, pl.ds(FL + f, NQ, stride=MSG), :]
            field = jnp.concatenate(
                [
                    jnp.concatenate([real, imag], axis=1),
                    jnp.concatenate([imag, -real], axis=1),
                ],
                axis=0,
            )
            high, low = split(field)
            both = dot(jnp.concatenate([high, low], axis=0), rhi[f])
            total = both[: 2 * NQ] + both[2 * NQ :] + dot(high, rlo[f])
            for s in range(NSD):
                columns = slice(s * LANES, (s + 1) * LANES)
                part[it, h, s, pl.ds(f, NQ, stride=MSG), :] = total[:NQ, columns]
                part[it, h, s, pl.ds(FL + f, NQ, stride=MSG), :] = total[NQ:, columns]
            return carry

        lax.fori_loop(0, FL, one, 0)
        for row in range(2):
            for half, dev in ((0, dev_p), (1, dev_m)):
                rs_msg(
                    part.at[it, h, row * NY + y2, rows_of(half)],
                    r1.at[it, h, row * 2 + half],
                    it, h, row * 2 + half, dev,
                )
        for row in range(2):
            rs_second(it, h, row, 0, 1)
            rs_second(it, h, row, 1, 0)

    def rs_middle(it, h):
        for row in range(2):
            for half, column in ((0, yp), (1, ym)):
                landed(r1.at[it, h, row * 2 + half], rs_recv.at[it, h, row * 2 + half])
                slot = row * NY + column
                part[it, h, slot, rows_of(half), :] += r1[it, h, row * 2 + half]
                rs_second(it, h, row, half, half)

    def rs_column(it, h, row, half):
        for direction in range(2):
            landed(
                r2.at[it, h, row * 2 + direction, rows_of(half)],
                rs_recv.at[it, h, 4 + row * 4 + direction * 2 + half],
            )
        slot = row * NY + y
        part[it, h, slot, rows_of(half), :] += (
            r2[it, h, row * 2, rows_of(half), :] + r2[it, h, row * 2 + 1, rows_of(half), :]
        )

    def rs_columns(it, h):
        for half in range(2):
            rs_column(it, h, z1, half)
            rs_msg(
                part.at[it, h, z1 * NY + y, rows_of(half)],
                rz.at[it, h, rows_of(half)],
                it, h, 12 + half, dev_z,
            )
        for half in range(2):
            rs_column(it, h, z, half)

    def rs_finish(it, h):
        for half in range(2):
            landed(rz.at[it, h, rows_of(half)], rs_recv.at[it, h, 12 + half])
            sbuf[it, h, 2, rows_of(half), :] = (
                part[it, h, src, rows_of(half), :] + rz[it, h, rows_of(half), :]
            )
        a2a_start(it, h, 2)

    def update(it, h):
        a2a_wait(it, h, 3)
        if it + 1 < ITERS:
            ag[it + 1, h, src] = ag[0, h, src] - rbuf[it, h, 3]
            ag_start(it + 1, h)
        else:
            for c in range(2):
                for f in range(FL):
                    rows = pl.ds(c * FL + f, NQ, stride=MSG)
                    down_out[c, f, pl.ds(h, NQ, stride=NC), :] = (
                        ag[0, h, src, rows, :] - rbuf[it, h, 3, rows, :]
                    )

    def write_upgoing(h):
        for c in range(2):
            for f in range(FL):
                up_out[c, f, pl.ds(h, NQ, stride=NC), :] = rbuf[
                    ITERS - 1, h, 1, pl.ds(c * FL + f, NQ, stride=MSG), :
                ]

    lay_out(0)
    pl.semaphore_wait(barrier, NFD - 1 + 3)
    ag_start(0, 0)
    lay_out(1)
    for f in range(3):
        prepare(f)
    ag_forward_z(0, 0)
    for f in range(3, 6):
        prepare(f)
    ag_forward_y(0, 0)
    for f in range(6, FL):
        prepare(f)
    ag_start(0, 1)
    ag_finish(0, 0)
    for it in range(ITERS):
        forward(it, 0)
        if it:
            update(it - 1, 1)
        ag_forward_z(it, 1)
        ag_forward_y(it, 1)
        window(it, 0, 0)
        ag_finish(it, 1)
        forward(it, 1)
        adjoint(it, 0)
        window(it, 1, 0)
        rs_middle(it, 0)
        rs_columns(it, 0)
        adjoint(it, 1)
        rs_finish(it, 0)
        if it == ITERS - 1:
            write_upgoing(0)
        rs_middle(it, 1)
        window(it, 0, 2)
        rs_columns(it, 1)
        update(it, 0)
        rs_finish(it, 1)
        if it + 1 < ITERS:
            ag_forward_z(it + 1, 0)
            ag_forward_y(it + 1, 0)
            window(it, 1, 2)
            ag_finish(it + 1, 0)
        else:
            write_upgoing(1)
            window(it, 1, 2)
            update(it, 1)

    for copy in pending:
        copy.wait_send()
    for it in range(ITERS):
        for h in range(NC):
            for k in range(4):
                a2a_sent(it, h, k)


def per_device(reflection, focusing, onsets):
    high, low = tables()
    vmem = pl.BlockSpec(memory_space=pltpu.VMEM)
    block = jax.ShapeDtypeStruct(focusing.shape, F32)
    return pl.pallas_call(
        kernel,
        out_shape=(block, block),
        in_specs=[pl.BlockSpec(memory_space=pl.ANY), vmem, vmem, vmem, vmem],
        out_specs=(vmem, vmem),
        scratch_shapes=[
            pltpu.VMEM((2, 2, LANES, 1024), F32),
            pltpu.VMEM((FL, 2 * LANES, 1024), BF16),
            pltpu.VMEM((FL, 2 * LANES, 1024), BF16),
            pltpu.VMEM((ITERS, NC, NSD, ROWS, LANES), F32),
            pltpu.VMEM((ITERS, NC, NSD, ROWS, LANES), F32),
            pltpu.VMEM((ITERS, NC, 4, HALF, LANES), F32),
            pltpu.VMEM((ITERS, NC, 4, ROWS, LANES), F32),
            pltpu.VMEM((ITERS, NC, ROWS, LANES), F32),
            pltpu.VMEM((ITERS, NC, 4, ROWS, LANES), F32),
            pltpu.VMEM((ITERS, NC, 4, ROWS, LANES), F32),
            pltpu.SemaphoreType.DMA((2,)),
            pltpu.SemaphoreType.DMA((ITERS, NC, 4)),
            pltpu.SemaphoreType.DMA((ITERS, NC, 4)),
            pltpu.SemaphoreType.DMA((ITERS, NC, 14)),
            pltpu.SemaphoreType.DMA((ITERS, NC, 14)),
            pltpu.SemaphoreType.DMA((ITERS, NC, 14)),
            pltpu.SemaphoreType.DMA((ITERS, NC, 14)),
        ],
        compiler_params=pltpu.CompilerParams(
            collective_id=0, has_side_effects=True, vmem_limit_bytes=56 * 1024 * 1024
        ),
        name="marchenko",
    )(reflection, focusing, onsets, jnp.asarray(high), jnp.asarray(low))


def solution(mesh):
    placed = (P(None, "freq", "src", None), P(None, "freq", None, "src"), P("freq", "src"))
    return jax.shard_map(
        per_device,
        mesh=mesh,
        in_specs=placed,
        out_specs=(P(None, "freq", None, "src"), P(None, "freq", None, "src")),
        check_vma=False,
    )
```

```python
import math

import jax
import jax.numpy as jnp
import ml_dtypes
import numpy as np
from jax import lax
from jax.experimental import pallas as pl
from jax.experimental.pallas import tpu as pltpu
from jax.sharding import PartitionSpec as P

ITERS = 2
NFD = 32
NSD = 8
NY = 4
FL = 8
NP = 64
NC = 4
NQ = NP // NC
NW = NC // 2
MSG = 2 * FL
ROWS = NQ * MSG
FROWS = 2 * NQ
HALF = ROWS // 2
TRACES = NFD * MSG
LANES = 128
NF = 256
ORDER = (
    "ags 0 0", "ags 0 1", "prep", "prep", "prep", "prep", "agz 0 0", "prep", "prep", "agz 0 1",
    "prep", "prep", "agy 0 0", "ags 0 2", "ags 0 3", "agy 0 1", "agz 0 2", "agf 0 0", "fwd 0 0",
    "agz 0 3", "win 0 0", "agf 0 1", "fwd 0 1", "agy 0 2", "agy 0 3", "adj 0 0", "win 0 1",
    "agf 0 2", "fwd 0 2", "rsm 0 0", "agf 0 3", "fwd 0 3", "adj 0 1", "rsc 0 0", "win 0 2",
    "win 0 3", "rsm 0 1", "rsf 0 0", "adj 0 2", "rsc 0 1", "adj 0 3", "win2 0 0", "rsm 0 2",
    "rsf 0 1", "rsm 0 3", "upd 0 0", "agz 1 0", "win2 0 1", "rsc 0 2", "rsc 0 3", "upd 0 1",
    "agz 1 1", "agy 1 0", "rsf 0 2", "rsf 0 3", "agy 1 1", "win2 0 2", "agf 1 0", "fwd 1 0",
    "win2 0 3", "agf 1 1", "fwd 1 1", "upd 0 2", "agz 1 2", "win 1 0", "upd 0 3", "agz 1 3",
    "agy 1 2", "win 1 1", "agy 1 3", "adj 1 0", "agf 1 2", "fwd 1 2", "agf 1 3", "fwd 1 3",
    "rsm 1 0", "adj 1 1", "win 1 2", "rsc 1 0", "win 1 3", "rsm 1 1", "adj 1 2", "rsf 1 0",
    "rsc 1 1", "adj 1 3", "win2 1 0", "rsm 1 2", "rsf 1 1", "rsm 1 3", "upd 1 0", "rsc 1 2",
    "win2 1 1", "rsc 1 3", "rsf 1 2", "upd 1 1", "rsf 1 3", "win2 1 2", "win2 1 3", "upd 1 2",
    "upd 1 3",
)
MESH = pl.DeviceIdType.MESH
F32 = jnp.float32
BF16 = jnp.bfloat16


def tables():
    samples = np.arange(NF)
    angles = (samples[:, None] * samples[None, :] % NF) * (2.0 * math.pi / NF)
    table = np.concatenate([np.cos(angles), np.sin(angles)], 0).astype(np.float32)
    high = table.astype(ml_dtypes.bfloat16)
    low = (table - high.astype(np.float32)).astype(ml_dtypes.bfloat16)
    return high, low


def split(values):
    high = values.astype(BF16)
    return high, (values - high.astype(F32)).astype(BF16)


def dot(left, right):
    return jnp.dot(left, right, preferred_element_type=F32)


def kernel(
    refl, foc, onsets, th, tl, down_out, up_out,
    rstage, rhi, rlo, thi, tlo, ag, part, r1, r2, rz, sfield, rfield, straces, rtraces,
    stage_sem, a2a_send, a2a_recv, ag_send, ag_recv, rs_send, rs_recv, entered,
):
    me = lax.axis_index("freq")
    src = lax.axis_index("src")
    z = src // NY
    y = lax.rem(src, NY)
    z1 = 1 - z
    yp = lax.rem(y + 1, NY)
    ym = lax.rem(y + NY - 1, NY)
    y2 = lax.rem(y + 2, NY)
    dev_p = (me, z * NY + yp)
    dev_m = (me, z * NY + ym)
    dev_z = (me, z1 * NY + y)

    z_hi, x, core = me // 8, lax.rem(me // 2, 4), lax.rem(me, 2)
    along_x = [(z_hi * 8 + lax.rem(x + k, 4) * 2 + core, src) for k in (1, 2, 3)]
    along_z = [(lax.rem(z_hi + k, 4) * 8 + x * 2 + core, src) for k in (1, 2, 3)]
    sibling = (z_hi * 8 + x * 2 + 1 - core, src)
    barrier = pltpu.get_barrier_semaphore()
    greeted = [dev_p, dev_m, dev_z, sibling, *along_x, *along_z]
    for dev in greeted:
        pl.semaphore_signal(barrier, inc=1, device_id=dev, device_id_type=MESH)

    def signal_round(number, devices):
        for dev in devices:
            pl.semaphore_signal(entered.at[number], inc=1, device_id=dev, device_id_type=MESH)

    def stage_copy(f):
        return pltpu.make_async_copy(refl.at[:, f], rstage.at[f % 2], stage_sem.at[f % 2])

    stage_copy(0).start()
    stage_copy(1).start()

    def lay_out(h):
        for c in range(2):
            for f in range(FL):
                ag[0, h, src, f * FROWS + c * NQ : f * FROWS + (c + 1) * NQ, :] = foc[
                    c, f, pl.ds(h, NQ, stride=NC), :
                ]

    def prepare(f):
        stage_copy(f).wait()
        for c in range(2):
            high, low = split(rstage[f % 2, c])
            rows = slice(c * LANES, (c + 1) * LANES)
            rhi[f, rows, :] = high
            rlo[f, rows, :] = low
            thi[f, :, rows] = high.T
            tlo[f, :, rows] = low.T
        if f + 2 < FL:
            stage_copy(f + 2).start()

    def rows_of(half):
        return pl.ds(half * HALF, HALF)

    def remote(source, target, send_sem, recv_sem, dev):
        copy = pltpu.make_async_remote_copy(
            source, target, send_sem, recv_sem, device_id=dev, device_id_type=MESH
        )
        copy.start()

    def landed(target, sem):
        pltpu.make_async_copy(target, target, sem).wait()

    def ag_msg(it, h, slot, half, number, dev):
        piece = ag.at[it, h, slot, rows_of(half)]
        remote(piece, piece, ag_send.at[it, h], ag_recv.at[it, h, number], dev)

    def ag_landed(it, h, slot, half, number):
        landed(ag.at[it, h, slot, rows_of(half)], ag_recv.at[it, h, number])

    def ag_start(it, h):
        for half in range(2):
            ag_msg(it, h, src, half, half, dev_z)
            ag_msg(it, h, src, half, 2 + half, dev_p)
            ag_msg(it, h, src, 1 - half, 4 + 1 - half, dev_m)

    def ag_forward_z(it, h):
        other = z1 * NY + y
        for half in range(2):
            ag_landed(it, h, other, half, half)
            ag_msg(it, h, other, half, 6 + half, dev_p)
            ag_msg(it, h, other, half, 8 + half, dev_m)

    def ag_forward_y(it, h):
        for row, base, number in ((z, 2, 10), (z1, 6, 12)):
            ag_landed(it, h, row * NY + ym, 0, base)
            ag_msg(it, h, row * NY + ym, 0, number, dev_p)
            ag_landed(it, h, row * NY + yp, 1, base + 3)
            ag_msg(it, h, row * NY + yp, 1, number + 1, dev_m)

    def ag_finish(it, h):
        for row, base, number in ((z, 2, 10), (z1, 6, 12)):
            ag_landed(it, h, row * NY + ym, 1, base + 1)
            ag_landed(it, h, row * NY + yp, 0, base + 2)
            ag_landed(it, h, row * NY + y2, 0, number)
            ag_landed(it, h, row * NY + y2, 1, number + 1)

    mine = me // NW
    lane = lax.rem(me, NW)
    own_field = pl.ds(pl.multiple_of(mine * MSG, MSG), MSG)
    own_traces = pl.ds(pl.multiple_of(me * MSG, MSG), MSG)

    def a2a_copy(source, target, it, h, k, peer):
        return pltpu.make_async_remote_copy(
            source, target, a2a_send.at[it, h, k], a2a_recv.at[it, h, k],
            device_id=(peer, src), device_id_type=MESH,
        )

    def to_windows(it, h, k):
        here = h // 2

        def send(step, carry):
            q = lax.rem(mine + step, NQ)
            a2a_copy(
                sfield.at[it, h, k // 2, pl.ds(pl.multiple_of(q * MSG, MSG), MSG)],
                rtraces.at[it, h, k // 2, own_traces],
                it, h, k, q * NW + here,
            ).start()
            return carry

        lax.fori_loop(1, NQ, send, 0)

        @pl.when(lane == here)
        def _():
            rtraces[it, h, k // 2, own_traces, :] = sfield[it, h, k // 2, own_field, :]

        if NW > 1:

            @pl.when(lane != here)
            def _():
                a2a_copy(
                    sfield.at[it, h, k // 2, own_field],
                    rtraces.at[it, h, k // 2, own_traces],
                    it, h, k, mine * NW + here,
                ).start()

    def from_windows(it, h, k):
        def send(step, carry):
            peer = lax.rem(me + step, NFD)
            a2a_copy(
                straces.at[it, h, k // 2, pl.ds(pl.multiple_of(peer * MSG, MSG), MSG)],
                rfield.at[it, h, k // 2, own_field],
                it, h, k, peer,
            ).start()
            return carry

        lax.fori_loop(1, NFD, send, 0)
        rfield[it, h, k // 2, own_field, :] = straces[it, h, k // 2, own_traces, :]

    def field_wait(buffer, it, h, k, sem):
        if NW > 1:

            @pl.when(lane != h // 2)
            def _():
                landed(buffer.at[it, h, k // 2], sem.at[it, h, k])

        @pl.when(lane == h // 2)
        def _():
            landed(buffer.at[it, h, k // 2, pl.ds(0, ROWS - MSG)], sem.at[it, h, k])

    def traces_wait(buffer, it, h, k, sem):
        landed(buffer.at[it, h, k // 2, pl.ds(0, TRACES - MSG)], sem.at[it, h, k])

    def forward(it, h):
        def one(f, carry):
            rows = pl.ds(pl.multiple_of(f * FROWS, FROWS), FROWS)
            field = jnp.concatenate([ag[it, h, s, rows, :] for s in range(NSD)], axis=1)
            high, low = split(field)
            both = dot(jnp.concatenate([high, low], axis=0), thi[f])
            total = both[: 2 * NQ] + both[2 * NQ :] + dot(high, tlo[f])
            sfield[it, h, 0, pl.ds(f, NQ, stride=MSG), :] = (
                total[:NQ, :LANES] - total[NQ:, LANES:]
            )
            sfield[it, h, 0, pl.ds(FL + f, NQ, stride=MSG), :] = (
                total[:NQ, LANES:] + total[NQ:, :LANES]
            )
            return carry

        lax.fori_loop(0, FL, one, 0, unroll=2)
        to_windows(it, h, 0)

    def transform(values):
        high, low = split(values)
        return dot(th[...], high) + (dot(tl[...], high) + dot(th[...], low))

    def window(it, h, k):
        traces_wait(rtraces, it, h, k, a2a_recv)
        received = rtraces[it, h, k // 2].reshape(NFD, 2, FL, LANES)
        spectra = jnp.concatenate(
            [received[:, 0].reshape(NF, LANES), received[:, 1].reshape(NF, LANES)], axis=1
        )
        times = transform(spectra)
        sample = lax.broadcasted_iota(jnp.int32, (NF, LANES), 0)
        nearest = jnp.minimum(sample, NF - sample)
        row = h % 2
        kept = jnp.where(nearest < onsets[row : row + 1, :], 1.0 / NF, 0.0).astype(F32)
        real = (times[:NF, :LANES] - times[NF:, LANES:]) * kept
        imag = (times[NF:, :LANES] + times[:NF, LANES:]) * kept
        back = transform(jnp.concatenate([real, imag], axis=1))
        back_real = back[:NF, :LANES] + back[NF:, LANES:]
        back_imag = back[:NF, LANES:] - back[NF:, :LANES]
        straces[it, h, k // 2] = jnp.concatenate(
            [back_real.reshape(NFD, 1, FL, LANES), back_imag.reshape(NFD, 1, FL, LANES)], axis=1
        ).reshape(TRACES, LANES)
        from_windows(it, h, k + 1)

    def windowed(it, h, k):
        if NW == 1:
            window(it, h, k)
        else:
            pl.when(lane == h // 2)(lambda: window(it, h, k))

    def rs_msg(source, target, it, h, number, dev):
        remote(source, target, rs_send.at[it, h], rs_recv.at[it, h, number], dev)

    def rs_second(it, h, row, direction, half):
        column, dev = ((yp, dev_p), (ym, dev_m))[direction]
        rs_msg(
            part.at[it, h, row * NY + column, rows_of(half)],
            r2.at[it, h, row * 2 + direction, rows_of(half)],
            it, h, 4 + row * 4 + direction * 2 + half, dev,
        )

    def adjoint(it, h):
        field_wait(rfield, it, h, 1, a2a_recv)

        def one(f, carry):
            real = rfield[it, h, 0, pl.ds(f, NQ, stride=MSG), :]
            imag = rfield[it, h, 0, pl.ds(FL + f, NQ, stride=MSG), :]
            field = jnp.concatenate(
                [
                    jnp.concatenate([real, imag], axis=1),
                    jnp.concatenate([imag, -real], axis=1),
                ],
                axis=0,
            )
            high, low = split(field)
            both = dot(jnp.concatenate([high, low], axis=0), rhi[f])
            total = both[: 2 * NQ] + both[2 * NQ :] + dot(high, rlo[f])
            rows = pl.ds(pl.multiple_of(f * FROWS, FROWS), FROWS)
            for s in range(NSD):
                part[it, h, s, rows, :] = total[:, s * LANES : (s + 1) * LANES]
            return carry

        lax.fori_loop(0, FL, one, 0, unroll=2)
        if it == ITERS - 1:
            write_upgoing(h)
        for row in range(2):
            for half, dev in ((0, dev_p), (1, dev_m)):
                rs_msg(
                    part.at[it, h, row * NY + y2, rows_of(half)],
                    r1.at[it, h, row * 2 + half],
                    it, h, row * 2 + half, dev,
                )
        for row in range(2):
            rs_second(it, h, row, 0, 1)
            rs_second(it, h, row, 1, 0)

    def rs_middle(it, h):
        for row in range(2):
            for half, column in ((0, yp), (1, ym)):
                landed(r1.at[it, h, row * 2 + half], rs_recv.at[it, h, row * 2 + half])
                slot = row * NY + column
                part[it, h, slot, rows_of(half), :] += r1[it, h, row * 2 + half]
                rs_second(it, h, row, half, half)

    def rs_column(it, h, row, half):
        for direction in range(2):
            landed(
                r2.at[it, h, row * 2 + direction, rows_of(half)],
                rs_recv.at[it, h, 4 + row * 4 + direction * 2 + half],
            )
        slot = row * NY + y
        part[it, h, slot, rows_of(half), :] += (
            r2[it, h, row * 2, rows_of(half), :] + r2[it, h, row * 2 + 1, rows_of(half), :]
        )

    def rs_columns(it, h):
        for half in range(2):
            rs_column(it, h, z1, half)
            rs_msg(
                part.at[it, h, z1 * NY + y, rows_of(half)],
                rz.at[it, h, rows_of(half)],
                it, h, 12 + half, dev_z,
            )
        for half in range(2):
            rs_column(it, h, z, half)

    def rs_finish(it, h):
        for half in range(2):
            landed(rz.at[it, h, rows_of(half)], rs_recv.at[it, h, 12 + half])
            for f in range(half * FL // 2, (half + 1) * FL // 2):
                for c in range(2):
                    rows = slice(f * FROWS + c * NQ, f * FROWS + (c + 1) * NQ)
                    sfield[it, h, 1, pl.ds(c * FL + f, NQ, stride=MSG), :] = (
                        part[it, h, src, rows, :] + rz[it, h, rows, :]
                    )
        to_windows(it, h, 2)

    def update(it, h):
        field_wait(rfield, it, h, 3, a2a_recv)
        for c in range(2):
            for f in range(FL):
                rows = slice(f * FROWS + c * NQ, f * FROWS + (c + 1) * NQ)
                field = (
                    ag[0, h, src, rows, :]
                    - rfield[it, h, 1, pl.ds(c * FL + f, NQ, stride=MSG), :]
                )
                if it + 1 < ITERS:
                    ag[it + 1, h, src, rows, :] = field
                else:
                    down_out[c, f, pl.ds(h, NQ, stride=NC), :] = field
        if it + 1 < ITERS:
            ag_start(it + 1, h)

    def write_upgoing(h):
        for c in range(2):
            for f in range(FL):
                up_out[c, f, pl.ds(h, NQ, stride=NC), :] = rfield[
                    ITERS - 1, h, 0, pl.ds(c * FL + f, NQ, stride=MSG), :
                ]

    steps = {
        "agz": ag_forward_z,
        "agy": ag_forward_y,
        "agf": ag_finish,
        "fwd": forward,
        "win": lambda it, h: windowed(it, h, 0),
        "adj": adjoint,
        "rsm": rs_middle,
        "rsc": rs_columns,
        "rsf": rs_finish,
        "win2": lambda it, h: windowed(it, h, 2),
        "upd": update,
    }

    lay_out(0)
    pl.semaphore_wait(barrier, len(greeted))
    signal_round(0, along_x)
    prepared = 0
    for step in ORDER:
        if step == "prep":
            prepare(prepared)
            prepared += 1
            if prepared == 2:
                pl.semaphore_wait(entered.at[0], 3)
                signal_round(1, along_z)
            if prepared == FL:
                pl.semaphore_wait(entered.at[1], 3)
            continue
        name, it, h = step.split()
        it, h = int(it), int(h)
        if name == "ags":
            if h > 0:
                lay_out(h)
            ag_start(it, h)
        else:
            steps[name](it, h)

    for it in range(ITERS):
        for h in range(NC):
            landed(ag.at[it, h, pl.ds(0, NSD - 1)], ag_send.at[it, h])
            landed(part.at[it, h, pl.ds(0, NSD - 1)], rs_send.at[it, h])
            for k in (0, 2):
                field_wait(sfield, it, h, k, a2a_send)
            for k in (1, 3):
                if NW == 1:
                    traces_wait(straces, it, h, k, a2a_send)
                else:
                    pl.when(lane == h // 2)(
                        lambda it=it, h=h, k=k: traces_wait(straces, it, h, k, a2a_send)
                    )


def per_device(reflection, focusing, onsets):
    high, low = tables()
    vmem = pl.BlockSpec(memory_space=pltpu.VMEM)
    block = jax.ShapeDtypeStruct(focusing.shape, F32)
    return pl.pallas_call(
        kernel,
        out_shape=(block, block),
        in_specs=[pl.BlockSpec(memory_space=pl.ANY), vmem, vmem, vmem, vmem],
        out_specs=(vmem, vmem),
        scratch_shapes=[
            pltpu.VMEM((2, 2, LANES, 1024), F32),
            pltpu.VMEM((FL, 2 * LANES, 1024), BF16),
            pltpu.VMEM((FL, 2 * LANES, 1024), BF16),
            pltpu.VMEM((FL, 1024, 2 * LANES), BF16),
            pltpu.VMEM((FL, 1024, 2 * LANES), BF16),
            pltpu.VMEM((ITERS, NC, NSD, ROWS, LANES), F32),
            pltpu.VMEM((ITERS, NC, NSD, ROWS, LANES), F32),
            pltpu.VMEM((ITERS, NC, 4, HALF, LANES), F32),
            pltpu.VMEM((ITERS, NC, 4, ROWS, LANES), F32),
            pltpu.VMEM((ITERS, NC, ROWS, LANES), F32),
            pltpu.VMEM((ITERS, NC, 2, ROWS, LANES), F32),
            pltpu.VMEM((ITERS, NC, 2, ROWS, LANES), F32),
            pltpu.VMEM((ITERS, NC, 2, TRACES, LANES), F32),
            pltpu.VMEM((ITERS, NC, 2, TRACES, LANES), F32),
            pltpu.SemaphoreType.DMA((2,)),
            pltpu.SemaphoreType.DMA((ITERS, NC, 4)),
            pltpu.SemaphoreType.DMA((ITERS, NC, 4)),
            pltpu.SemaphoreType.DMA((ITERS, NC)),
            pltpu.SemaphoreType.DMA((ITERS, NC, 14)),
            pltpu.SemaphoreType.DMA((ITERS, NC)),
            pltpu.SemaphoreType.DMA((ITERS, NC, 14)),
            pltpu.SemaphoreType.REGULAR((2,)),
        ],
        compiler_params=pltpu.CompilerParams(
            collective_id=0, has_side_effects=True, vmem_limit_bytes=62 * 1024 * 1024
        ),
        name="marchenko",
    )(reflection, focusing, onsets, jnp.asarray(high), jnp.asarray(low))


def solution(mesh):
    placed = (P(None, "freq", "src", None), P(None, "freq", None, "src"), P("freq", "src"))
    return jax.shard_map(
        per_device,
        mesh=mesh,
        in_specs=placed,
        out_specs=(P(None, "freq", None, "src"), P(None, "freq", None, "src")),
        check_vma=False,
    )
```

```python
import math

import jax
import jax.numpy as jnp
import ml_dtypes
import numpy as np
from jax import lax
from jax.experimental import pallas as pl
from jax.experimental.pallas import tpu as pltpu
from jax.sharding import PartitionSpec as P

ITERS = 2
NFD = 32
NSD = 8
NY = 4
FL = 8
NP = 64
NC = 4
NQ = NP // NC
NW = NC // 2
MSG = 2 * FL
ROWS = NQ * MSG
FROWS = 2 * NQ
HALF = ROWS // 2
TRACES = NFD * MSG
LANES = 128
NF = 256
ORDER = (
    "ags 0 0", "ags 0 1", "prep", "prep", "prep", "prep", "prep", "agz 0 0", "prep", "agy 0 0",
    "prep", "prep", "ags 0 2", "agz 0 1", "agf 0 0", "fwd 0 0", "agy 0 1", "agz 0 2", "ags 0 3",
    "agf 0 1", "fwd 0 1", "agy 0 2", "agz 0 3", "win 0 0", "agf 0 2", "fwd 0 2", "agy 0 3",
    "win 0 1", "adj 0 0", "agf 0 3", "fwd 0 3", "rsm 0 0", "win 0 2", "adj 0 1", "rsc 0 0",
    "win 0 3", "rsm 0 1", "rsf 0 0", "adj 0 2", "rsc 0 1", "rsm 0 2", "rsf 0 1", "win2 0 0",
    "rsc 0 2", "adj 0 3", "win2 0 1", "rsm 0 3", "rsf 0 2", "upd 0 0", "upd 0 1", "rsc 0 3",
    "win2 0 2", "agz 1 1", "agy 1 1", "agz 1 0", "rsf 0 3", "agf 1 1", "fwd 1 1", "agy 1 0",
    "upd 0 2", "agf 1 0", "win2 0 3", "fwd 1 0", "agz 1 2", "agy 1 2", "win 1 1", "upd 0 3",
    "agf 1 2", "fwd 1 2", "agz 1 3", "win 1 0", "agy 1 3", "adj 1 1", "agf 1 3", "fwd 1 3",
    "rsm 1 1", "win 1 2", "adj 1 0", "rsc 1 1", "win 1 3", "rsm 1 0", "rsf 1 1", "adj 1 2",
    "rsc 1 0", "rsf 1 0", "rsm 1 2", "adj 1 3", "rsc 1 2", "win2 1 1", "rsm 1 3", "rsf 1 2",
    "rsc 1 3", "rsf 1 3", "win2 1 2", "win2 1 0", "upd 1 1", "win2 1 3", "upd 1 2", "upd 1 0",
    "upd 1 3",
)
MESH = pl.DeviceIdType.MESH
F32 = jnp.float32
BF16 = jnp.bfloat16


def tables():
    samples = np.arange(NF)
    angles = (samples[:, None] * samples[None, :] % NF) * (2.0 * math.pi / NF)
    table = np.concatenate([np.cos(angles), np.sin(angles)], 0).astype(np.float32)
    high = table.astype(ml_dtypes.bfloat16)
    low = (table - high.astype(np.float32)).astype(ml_dtypes.bfloat16)
    return high, low


def split(values):
    high = values.astype(BF16)
    return high, (values - high.astype(F32)).astype(BF16)


def dot(left, right):
    return jnp.dot(left, right, preferred_element_type=F32)


def kernel(
    refl, foc, onsets, th, tl, out,
    rstage, rhi, rlo, thi, tlo, ag, part, r1, r2, rz, sfield, rfield, straces, rtraces,
    stage_sem, a2a_send, a2a_recv, ag_send, ag_recv, rs_send, rs_recv, entered,
):
    me = lax.axis_index("freq")
    src = lax.axis_index("src")
    z = src // NY
    y = lax.rem(src, NY)
    z1 = 1 - z
    yp = lax.rem(y + 1, NY)
    ym = lax.rem(y + NY - 1, NY)
    y2 = lax.rem(y + 2, NY)
    dev_p = (me, z * NY + yp)
    dev_m = (me, z * NY + ym)
    dev_z = (me, z1 * NY + y)

    z_hi, x, core = me // 8, lax.rem(me // 2, 4), lax.rem(me, 2)
    along_x = [(z_hi * 8 + lax.rem(x + k, 4) * 2 + core, src) for k in (1, 2, 3)]
    along_z = [(lax.rem(z_hi + k, 4) * 8 + x * 2 + core, src) for k in (1, 2, 3)]
    sibling = (z_hi * 8 + x * 2 + 1 - core, src)
    barrier = pltpu.get_barrier_semaphore()
    greeted = [dev_p, dev_m, dev_z, sibling, *along_x, *along_z]
    for dev in greeted:
        pl.semaphore_signal(barrier, inc=1, device_id=dev, device_id_type=MESH)

    def signal_round(number, devices):
        for dev in devices:
            pl.semaphore_signal(entered.at[number], inc=1, device_id=dev, device_id_type=MESH)

    def stage_copy(f):
        return pltpu.make_async_copy(refl.at[:, f], rstage.at[f % 2], stage_sem.at[f % 2])

    stage_copy(0).start()
    stage_copy(1).start()

    def lay_out(h):
        for c in range(2):
            for f in range(FL):
                ag[0, h, src, f * FROWS + c * NQ : f * FROWS + (c + 1) * NQ, :] = foc[
                    c, f, pl.ds(h, NQ, stride=NC), :
                ]

    def prepare(f):
        stage_copy(f).wait()
        for c in range(2):
            high, low = split(rstage[f % 2, c])
            rows = slice(c * LANES, (c + 1) * LANES)
            rhi[f, rows, :] = high
            rlo[f, rows, :] = low
            thi[f, :, rows] = high.T
            tlo[f, :, rows] = low.T
        if f + 2 < FL:
            stage_copy(f + 2).start()

    def rows_of(half):
        return pl.ds(half * HALF, HALF)

    def remote(source, target, send_sem, recv_sem, dev):
        copy = pltpu.make_async_remote_copy(
            source, target, send_sem, recv_sem, device_id=dev, device_id_type=MESH
        )
        copy.start()

    def landed(target, sem):
        pltpu.make_async_copy(target, target, sem).wait()

    def ag_msg(it, h, slot, half, number, dev):
        piece = ag.at[it, h, slot, rows_of(half)]
        remote(piece, piece, ag_send.at[it, h], ag_recv.at[it, h, number], dev)

    def ag_landed(it, h, slot, half, number):
        landed(ag.at[it, h, slot, rows_of(half)], ag_recv.at[it, h, number])

    def ag_start(it, h):
        for half in range(2):
            ag_msg(it, h, src, half, half, dev_z)
            ag_msg(it, h, src, half, 2 + half, dev_p)
            ag_msg(it, h, src, 1 - half, 4 + 1 - half, dev_m)

    def ag_forward_z(it, h):
        other = z1 * NY + y
        for half in range(2):
            ag_landed(it, h, other, half, half)
            ag_msg(it, h, other, half, 6 + half, dev_p)
            ag_msg(it, h, other, half, 8 + half, dev_m)

    def ag_forward_y(it, h):
        for row, base, number in ((z, 2, 10), (z1, 6, 12)):
            ag_landed(it, h, row * NY + ym, 0, base)
            ag_msg(it, h, row * NY + ym, 0, number, dev_p)
            ag_landed(it, h, row * NY + yp, 1, base + 3)
            ag_msg(it, h, row * NY + yp, 1, number + 1, dev_m)

    def ag_finish(it, h):
        for row, base, number in ((z, 2, 10), (z1, 6, 12)):
            ag_landed(it, h, row * NY + ym, 1, base + 1)
            ag_landed(it, h, row * NY + yp, 0, base + 2)
            ag_landed(it, h, row * NY + y2, 0, number)
            ag_landed(it, h, row * NY + y2, 1, number + 1)

    mine = me // NW
    lane = lax.rem(me, NW)
    own_field = pl.ds(pl.multiple_of(mine * MSG, MSG), MSG)
    own_traces = pl.ds(pl.multiple_of(me * MSG, MSG), MSG)

    def a2a_copy(source, target, it, h, k, peer):
        return pltpu.make_async_remote_copy(
            source, target, a2a_send.at[it, h, k], a2a_recv.at[it, h, k],
            device_id=(peer, src), device_id_type=MESH,
        )

    def to_windows(it, h, k):
        here = h // 2

        def send(step, carry):
            q = lax.rem(mine + step, NQ)
            a2a_copy(
                sfield.at[it, h, k // 2, pl.ds(pl.multiple_of(q * MSG, MSG), MSG)],
                rtraces.at[it, h, k // 2, own_traces],
                it, h, k, q * NW + here,
            ).start()
            return carry

        lax.fori_loop(1, NQ, send, 0)

        @pl.when(lane == here)
        def _():
            rtraces[it, h, k // 2, own_traces, :] = sfield[it, h, k // 2, own_field, :]

        if NW > 1:

            @pl.when(lane != here)
            def _():
                a2a_copy(
                    sfield.at[it, h, k // 2, own_field],
                    rtraces.at[it, h, k // 2, own_traces],
                    it, h, k, mine * NW + here,
                ).start()

    def from_windows(it, h, k):
        def send(step, carry):
            peer = lax.rem(me + step, NFD)
            a2a_copy(
                straces.at[it, h, k // 2, pl.ds(pl.multiple_of(peer * MSG, MSG), MSG)],
                rfield.at[it, h, k // 2, own_field],
                it, h, k, peer,
            ).start()
            return carry

        lax.fori_loop(1, NFD, send, 0)
        rfield[it, h, k // 2, own_field, :] = straces[it, h, k // 2, own_traces, :]

    def field_wait(buffer, it, h, k, sem):
        if NW > 1:

            @pl.when(lane != h // 2)
            def _():
                landed(buffer.at[it, h, k // 2], sem.at[it, h, k])

        @pl.when(lane == h // 2)
        def _():
            landed(buffer.at[it, h, k // 2, pl.ds(0, ROWS - MSG)], sem.at[it, h, k])

    def traces_wait(buffer, it, h, k, sem):
        landed(buffer.at[it, h, k // 2, pl.ds(0, TRACES - MSG)], sem.at[it, h, k])

    def forward(it, h):
        def one(f, carry):
            rows = pl.ds(pl.multiple_of(f * FROWS, FROWS), FROWS)
            field = jnp.concatenate([ag[it, h, s, rows, :] for s in range(NSD)], axis=1)
            high, low = split(field)
            both = dot(jnp.concatenate([high, low], axis=0), thi[f])
            total = both[: 2 * NQ] + both[2 * NQ :] + dot(high, tlo[f])
            sfield[it, h, 0, pl.ds(f, NQ, stride=MSG), :] = (
                total[:NQ, :LANES] - total[NQ:, LANES:]
            )
            sfield[it, h, 0, pl.ds(FL + f, NQ, stride=MSG), :] = (
                total[:NQ, LANES:] + total[NQ:, :LANES]
            )
            return carry

        lax.fori_loop(0, FL, one, 0, unroll=2)
        to_windows(it, h, 0)

    def transform(values):
        high, low = split(values)
        return dot(th[...], high) + (dot(tl[...], high) + dot(th[...], low))

    def window(it, h, k):
        traces_wait(rtraces, it, h, k, a2a_recv)
        received = rtraces[it, h, k // 2].reshape(NFD, 2, FL, LANES)
        spectra = jnp.concatenate(
            [received[:, 0].reshape(NF, LANES), received[:, 1].reshape(NF, LANES)], axis=1
        )
        times = transform(spectra)
        sample = lax.broadcasted_iota(jnp.int32, (NF, LANES), 0)
        nearest = jnp.minimum(sample, NF - sample)
        row = h % 2
        kept = jnp.where(nearest < onsets[row : row + 1, :], 1.0 / NF, 0.0).astype(F32)
        real = (times[:NF, :LANES] - times[NF:, LANES:]) * kept
        imag = (times[NF:, :LANES] + times[:NF, LANES:]) * kept
        back = transform(jnp.concatenate([real, imag], axis=1))
        back_real = back[:NF, :LANES] + back[NF:, LANES:]
        back_imag = back[:NF, LANES:] - back[NF:, :LANES]
        straces[it, h, k // 2] = jnp.concatenate(
            [back_real.reshape(NFD, 1, FL, LANES), back_imag.reshape(NFD, 1, FL, LANES)], axis=1
        ).reshape(TRACES, LANES)
        from_windows(it, h, k + 1)

    def windowed(it, h, k):
        if NW == 1:
            window(it, h, k)
        else:
            pl.when(lane == h // 2)(lambda: window(it, h, k))

    def rs_msg(source, target, it, h, number, dev):
        remote(source, target, rs_send.at[it, h], rs_recv.at[it, h, number], dev)

    def rs_second(it, h, row, direction, half):
        column, dev = ((yp, dev_p), (ym, dev_m))[direction]
        rs_msg(
            part.at[it, h, row * NY + column, rows_of(half)],
            r2.at[it, h, row * 2 + direction, rows_of(half)],
            it, h, 4 + row * 4 + direction * 2 + half, dev,
        )

    def adjoint(it, h):
        field_wait(rfield, it, h, 1, a2a_recv)

        def one(f, carry):
            real = rfield[it, h, 0, pl.ds(f, NQ, stride=MSG), :]
            imag = rfield[it, h, 0, pl.ds(FL + f, NQ, stride=MSG), :]
            field = jnp.concatenate(
                [
                    jnp.concatenate([real, imag], axis=1),
                    jnp.concatenate([imag, -real], axis=1),
                ],
                axis=0,
            )
            high, low = split(field)
            both = dot(jnp.concatenate([high, low], axis=0), rhi[f])
            total = both[: 2 * NQ] + both[2 * NQ :] + dot(high, rlo[f])
            rows = pl.ds(pl.multiple_of(f * FROWS, FROWS), FROWS)
            for s in range(NSD):
                part[it, h, s, rows, :] = total[:, s * LANES : (s + 1) * LANES]
            return carry

        lax.fori_loop(0, FL, one, 0, unroll=2)
        if it == ITERS - 1:
            write_upgoing(h)
        for row in range(2):
            for half, dev in ((0, dev_p), (1, dev_m)):
                rs_msg(
                    part.at[it, h, row * NY + y2, rows_of(half)],
                    r1.at[it, h, row * 2 + half],
                    it, h, row * 2 + half, dev,
                )
        for row in range(2):
            rs_second(it, h, row, 0, 1)
            rs_second(it, h, row, 1, 0)

    def rs_middle(it, h):
        for row in range(2):
            for half, column in ((0, yp), (1, ym)):
                landed(r1.at[it, h, row * 2 + half], rs_recv.at[it, h, row * 2 + half])
                slot = row * NY + column
                part[it, h, slot, rows_of(half), :] += r1[it, h, row * 2 + half]
                rs_second(it, h, row, half, half)

    def rs_column(it, h, row, half):
        for direction in range(2):
            landed(
                r2.at[it, h, row * 2 + direction, rows_of(half)],
                rs_recv.at[it, h, 4 + row * 4 + direction * 2 + half],
            )
        slot = row * NY + y
        part[it, h, slot, rows_of(half), :] += (
            r2[it, h, row * 2, rows_of(half), :] + r2[it, h, row * 2 + 1, rows_of(half), :]
        )

    def rs_columns(it, h):
        for half in range(2):
            rs_column(it, h, z1, half)
            rs_msg(
                part.at[it, h, z1 * NY + y, rows_of(half)],
                rz.at[it, h, rows_of(half)],
                it, h, 12 + half, dev_z,
            )
        for half in range(2):
            rs_column(it, h, z, half)

    def rs_finish(it, h):
        for half in range(2):
            landed(rz.at[it, h, rows_of(half)], rs_recv.at[it, h, 12 + half])
            for f in range(half * FL // 2, (half + 1) * FL // 2):
                for c in range(2):
                    rows = slice(f * FROWS + c * NQ, f * FROWS + (c + 1) * NQ)
                    sfield[it, h, 1, pl.ds(c * FL + f, NQ, stride=MSG), :] = (
                        part[it, h, src, rows, :] + rz[it, h, rows, :]
                    )
        to_windows(it, h, 2)

    def update(it, h):
        field_wait(rfield, it, h, 3, a2a_recv)
        for c in range(2):
            for f in range(FL):
                rows = slice(f * FROWS + c * NQ, f * FROWS + (c + 1) * NQ)
                field = rfield[it, h, 1, pl.ds(c * FL + f, NQ, stride=MSG), :]
                if it + 1 < ITERS:
                    ag[it + 1, h, src, rows, :] = ag[0, h, src, rows, :] - field
                else:
                    out[0, c, f, pl.ds(h, NQ, stride=NC), :] = field
        if it + 1 < ITERS:
            ag_start(it + 1, h)

    def write_upgoing(h):
        for c in range(2):
            for f in range(FL):
                out[1, c, f, pl.ds(h, NQ, stride=NC), :] = rfield[
                    ITERS - 1, h, 0, pl.ds(c * FL + f, NQ, stride=MSG), :
                ]

    steps = {
        "agz": ag_forward_z,
        "agy": ag_forward_y,
        "agf": ag_finish,
        "fwd": forward,
        "win": lambda it, h: windowed(it, h, 0),
        "adj": adjoint,
        "rsm": rs_middle,
        "rsc": rs_columns,
        "rsf": rs_finish,
        "win2": lambda it, h: windowed(it, h, 2),
        "upd": update,
    }

    lay_out(0)
    pl.semaphore_wait(barrier, len(greeted))
    signal_round(0, along_x)
    prepared = 0
    for step in ORDER:
        if step == "prep":
            prepare(prepared)
            prepared += 1
            if prepared == 2:
                pl.semaphore_wait(entered.at[0], 3)
                signal_round(1, along_z)
            if prepared == FL:
                pl.semaphore_wait(entered.at[1], 3)
            continue
        name, it, h = step.split()
        it, h = int(it), int(h)
        if name == "ags":
            if h > 0:
                lay_out(h)
            ag_start(it, h)
        else:
            steps[name](it, h)

    for it in range(ITERS):
        for h in range(NC):
            landed(ag.at[it, h, pl.ds(0, NSD - 1)], ag_send.at[it, h])
            landed(part.at[it, h, pl.ds(0, NSD - 1)], rs_send.at[it, h])
            for k in (0, 2):
                field_wait(sfield, it, h, k, a2a_send)
            for k in (1, 3):
                if NW == 1:
                    traces_wait(straces, it, h, k, a2a_send)
                else:
                    pl.when(lane == h // 2)(
                        lambda it=it, h=h, k=k: traces_wait(straces, it, h, k, a2a_send)
                    )


def per_device(reflection, focusing, onsets):
    high, low = tables()
    vmem = pl.BlockSpec(memory_space=pltpu.VMEM)
    fields = pl.pallas_call(
        kernel,
        out_shape=jax.ShapeDtypeStruct((2, *focusing.shape), F32),
        in_specs=[pl.BlockSpec(memory_space=pl.ANY), vmem, vmem, vmem, vmem],
        out_specs=vmem,
        scratch_shapes=[
            pltpu.VMEM((2, 2, LANES, 1024), F32),
            pltpu.VMEM((FL, 2 * LANES, 1024), BF16),
            pltpu.VMEM((FL, 2 * LANES, 1024), BF16),
            pltpu.VMEM((FL, 1024, 2 * LANES), BF16),
            pltpu.VMEM((FL, 1024, 2 * LANES), BF16),
            pltpu.VMEM((ITERS, NC, NSD, ROWS, LANES), F32),
            pltpu.VMEM((ITERS, NC, NSD, ROWS, LANES), F32),
            pltpu.VMEM((ITERS, NC, 4, HALF, LANES), F32),
            pltpu.VMEM((ITERS, NC, 4, ROWS, LANES), F32),
            pltpu.VMEM((ITERS, NC, ROWS, LANES), F32),
            pltpu.VMEM((ITERS, NC, 2, ROWS, LANES), F32),
            pltpu.VMEM((ITERS, NC, 2, ROWS, LANES), F32),
            pltpu.VMEM((ITERS, NC, 2, TRACES, LANES), F32),
            pltpu.VMEM((ITERS, NC, 2, TRACES, LANES), F32),
            pltpu.SemaphoreType.DMA((2,)),
            pltpu.SemaphoreType.DMA((ITERS, NC, 4)),
            pltpu.SemaphoreType.DMA((ITERS, NC, 4)),
            pltpu.SemaphoreType.DMA((ITERS, NC)),
            pltpu.SemaphoreType.DMA((ITERS, NC, 14)),
            pltpu.SemaphoreType.DMA((ITERS, NC)),
            pltpu.SemaphoreType.DMA((ITERS, NC, 14)),
            pltpu.SemaphoreType.REGULAR((2,)),
        ],
        compiler_params=pltpu.CompilerParams(
            collective_id=0, has_side_effects=True, vmem_limit_bytes=62 * 1024 * 1024
        ),
        name="marchenko",
    )(reflection, focusing, onsets, jnp.asarray(high), jnp.asarray(low))
    return focusing - fields[0], fields[1]


def solution(mesh):
    placed = (P(None, "freq", "src", None), P(None, "freq", None, "src"), P("freq", "src"))
    return jax.shard_map(
        per_device,
        mesh=mesh,
        in_specs=placed,
        out_specs=(P(None, "freq", None, "src"), P(None, "freq", None, "src")),
        check_vma=False,
    )
```

```python
import math

import jax
import jax.numpy as jnp
import ml_dtypes
import numpy as np
from jax import lax
from jax.experimental import pallas as pl
from jax.experimental.pallas import tpu as pltpu
from jax.sharding import PartitionSpec as P

ITERS = 2
NFD = 32
NSD = 8
NY = 4
FL = 8
NP = 64
NC = 4
NQ = NP // NC
NW = NC // 2
MSG = 2 * FL
ROWS = NQ * MSG
FROWS = 2 * NQ
HALF = ROWS // 2
TRACES = NFD * MSG
LANES = 128
NF = 256
ORDER = (
    "ags 0 1", "ags 0 0", "prep", "prep", "prep", "prep", "agz 0 1", "prep", "agz 0 0",
    "agy 0 0", "agy 0 1", "ags 0 2", "ags 0 3", "prep", "prep", "prep", "agz 0 2", "agf 0 0",
    "fwd 0 0", "agf 0 1", "fwd 0 1", "win 0 0", "agy 0 2", "agz 0 3", "win 0 1", "agf 0 2",
    "fwd 0 2", "agy 0 3", "adj 0 0", "agf 0 3", "fwd 0 3", "rsm 0 0", "adj 0 1", "win 0 2",
    "rsc 0 0", "win 0 3", "rsm 0 1", "rsf 0 0", "adj 0 2", "rsc 0 1", "rsm 0 2", "rsf 0 1",
    "win2 0 0", "adj 0 3", "rsc 0 2", "win2 0 1", "rsm 0 3", "rsf 0 2", "upd 0 0", "rsc 0 3",
    "agz 1 0", "win2 0 2", "agy 1 0", "upd 0 1", "agf 1 0", "rsf 0 3", "fwd 1 0", "agz 1 1",
    "upd 0 2", "agy 1 1", "win2 0 3", "agz 1 2", "win 1 0", "agf 1 1", "fwd 1 1", "agy 1 2",
    "upd 0 3", "agf 1 2", "fwd 1 2", "agz 1 3", "win 1 1", "agy 1 3", "adj 1 0", "agf 1 3",
    "fwd 1 3", "win 1 2", "rsm 1 0", "adj 1 1", "rsc 1 0", "win 1 3", "rsm 1 1", "adj 1 2",
    "rsf 1 0", "rsc 1 1", "rsm 1 2", "adj 1 3", "rsf 1 1", "rsc 1 2", "win2 1 0", "rsm 1 3",
    "rsf 1 2", "rsc 1 3", "rsf 1 3", "upd 1 0", "win2 1 2", "win2 1 1", "win2 1 3", "upd 1 2",
    "upd 1 1", "upd 1 3",
)
MESH = pl.DeviceIdType.MESH
F32 = jnp.float32
BF16 = jnp.bfloat16


def tables():
    samples = np.arange(NF)
    angles = (samples[:, None] * samples[None, :] % NF) * (2.0 * math.pi / NF)
    table = np.concatenate([np.cos(angles), np.sin(angles)], 0).astype(np.float32)
    high = table.astype(ml_dtypes.bfloat16)
    low = (table - high.astype(np.float32)).astype(ml_dtypes.bfloat16)
    return high, low


def split(values):
    high = values.astype(BF16)
    return high, (values - high.astype(F32)).astype(BF16)


def dot(left, right):
    return jnp.dot(left, right, preferred_element_type=F32)


def kernel(
    refl, foc, onsets, th, tl, out,
    rstage, rhi, rlo, thi, tlo, ag, part, r1, r2, rz, sfield, rfield, straces, rtraces,
    stage_sem, a2a_send, a2a_recv, ag_send, ag_recv, rs_send, rs_recv, entered,
):
    me = lax.axis_index("freq")
    src = lax.axis_index("src")
    z = src // NY
    y = lax.rem(src, NY)
    z1 = 1 - z
    yp = lax.rem(y + 1, NY)
    ym = lax.rem(y + NY - 1, NY)
    y2 = lax.rem(y + 2, NY)
    dev_p = (me, z * NY + yp)
    dev_m = (me, z * NY + ym)
    dev_z = (me, z1 * NY + y)

    z_hi, x, core = me // 8, lax.rem(me // 2, 4), lax.rem(me, 2)
    along_x = [(z_hi * 8 + lax.rem(x + k, 4) * 2 + core, src) for k in (1, 2, 3)]
    along_z = [(lax.rem(z_hi + k, 4) * 8 + x * 2 + core, src) for k in (1, 2, 3)]
    sibling = (z_hi * 8 + x * 2 + 1 - core, src)
    barrier = pltpu.get_barrier_semaphore()
    greeted = [dev_p, dev_m, dev_z, sibling, *along_x, *along_z]
    for dev in greeted:
        pl.semaphore_signal(barrier, inc=1, device_id=dev, device_id_type=MESH)

    def signal_round(number, devices):
        for dev in devices:
            pl.semaphore_signal(entered.at[number], inc=1, device_id=dev, device_id_type=MESH)

    def stage_copy(f):
        return pltpu.make_async_copy(refl.at[:, f], rstage.at[f % 2], stage_sem.at[f % 2])

    stage_copy(0).start()
    stage_copy(1).start()

    def lay_out(h):
        for c in range(2):
            for f in range(FL):
                ag[0, h, src, f * FROWS + c * NQ : f * FROWS + (c + 1) * NQ, :] = foc[
                    c, f, pl.ds(h, NQ, stride=NC), :
                ]

    def prepare(f):
        stage_copy(f).wait()
        for c in range(2):
            high, low = split(rstage[f % 2, c])
            rows = slice(c * LANES, (c + 1) * LANES)
            rhi[f, rows, :] = high
            rlo[f, rows, :] = low
            thi[f, :, rows] = high.T
            tlo[f, :, rows] = low.T
        if f + 2 < FL:
            stage_copy(f + 2).start()

    def rows_of(half):
        return pl.ds(half * HALF, HALF)

    def remote(source, target, send_sem, recv_sem, dev):
        copy = pltpu.make_async_remote_copy(
            source, target, send_sem, recv_sem, device_id=dev, device_id_type=MESH
        )
        copy.start()

    def landed(target, sem):
        pltpu.make_async_copy(target, target, sem).wait()

    def ag_msg(it, h, slot, half, number, dev):
        piece = ag.at[it, h, slot, rows_of(half)]
        remote(piece, piece, ag_send.at[it, h], ag_recv.at[it, h, number], dev)

    def ag_landed(it, h, slot, half, number):
        landed(ag.at[it, h, slot, rows_of(half)], ag_recv.at[it, h, number])

    def ag_start(it, h):
        for half in range(2):
            ag_msg(it, h, src, half, half, dev_z)
            ag_msg(it, h, src, half, 2 + half, dev_p)
            ag_msg(it, h, src, 1 - half, 4 + 1 - half, dev_m)

    def ag_forward_z(it, h):
        other = z1 * NY + y
        for half in range(2):
            ag_landed(it, h, other, half, half)
            ag_msg(it, h, other, half, 6 + half, dev_p)
            ag_msg(it, h, other, half, 8 + half, dev_m)

    def ag_forward_y(it, h):
        for row, base, number in ((z, 2, 10), (z1, 6, 12)):
            ag_landed(it, h, row * NY + ym, 0, base)
            ag_msg(it, h, row * NY + ym, 0, number, dev_p)
            ag_landed(it, h, row * NY + yp, 1, base + 3)
            ag_msg(it, h, row * NY + yp, 1, number + 1, dev_m)

    def ag_finish(it, h):
        for row, base, number in ((z, 2, 10), (z1, 6, 12)):
            ag_landed(it, h, row * NY + ym, 1, base + 1)
            ag_landed(it, h, row * NY + yp, 0, base + 2)
            ag_landed(it, h, row * NY + y2, 0, number)
            ag_landed(it, h, row * NY + y2, 1, number + 1)

    mine = me // NW
    lane = lax.rem(me, NW)
    own_field = pl.ds(pl.multiple_of(mine * MSG, MSG), MSG)
    own_traces = pl.ds(pl.multiple_of(me * MSG, MSG), MSG)

    def a2a_copy(source, target, it, h, k, peer):
        return pltpu.make_async_remote_copy(
            source, target, a2a_send.at[it, h, k], a2a_recv.at[it, h, k],
            device_id=(peer, src), device_id_type=MESH,
        )

    def to_windows(it, h, k):
        here = h // 2

        def send(step, carry):
            q = lax.rem(mine + step, NQ)
            a2a_copy(
                sfield.at[it, h, k // 2, pl.ds(pl.multiple_of(q * MSG, MSG), MSG)],
                rtraces.at[it, h, k // 2, own_traces],
                it, h, k, q * NW + here,
            ).start()
            return carry

        lax.fori_loop(1, NQ, send, 0)

        @pl.when(lane == here)
        def _():
            rtraces[it, h, k // 2, own_traces, :] = sfield[it, h, k // 2, own_field, :]

        if NW > 1:

            @pl.when(lane != here)
            def _():
                a2a_copy(
                    sfield.at[it, h, k // 2, own_field],
                    rtraces.at[it, h, k // 2, own_traces],
                    it, h, k, mine * NW + here,
                ).start()

    def from_windows(it, h, k):
        def send(step, carry):
            peer = lax.rem(me + step, NFD)
            a2a_copy(
                straces.at[it, h, k // 2, pl.ds(pl.multiple_of(peer * MSG, MSG), MSG)],
                rfield.at[it, h, k // 2, own_field],
                it, h, k, peer,
            ).start()
            return carry

        lax.fori_loop(1, NFD, send, 0)
        rfield[it, h, k // 2, own_field, :] = straces[it, h, k // 2, own_traces, :]

    def field_wait(buffer, it, h, k, sem):
        if NW > 1:

            @pl.when(lane != h // 2)
            def _():
                landed(buffer.at[it, h, k // 2], sem.at[it, h, k])

        @pl.when(lane == h // 2)
        def _():
            landed(buffer.at[it, h, k // 2, pl.ds(0, ROWS - MSG)], sem.at[it, h, k])

    def traces_wait(buffer, it, h, k, sem):
        landed(buffer.at[it, h, k // 2, pl.ds(0, TRACES - MSG)], sem.at[it, h, k])

    def forward(it, h):
        def one(f, carry):
            rows = pl.ds(pl.multiple_of(f * FROWS, FROWS), FROWS)
            field = jnp.concatenate([ag[it, h, s, rows, :] for s in range(NSD)], axis=1)
            high, low = split(field)
            both = dot(jnp.concatenate([high, low], axis=0), thi[f])
            total = both[: 2 * NQ] + both[2 * NQ :] + dot(high, tlo[f])
            sfield[it, h, 0, pl.ds(f, NQ, stride=MSG), :] = (
                total[:NQ, :LANES] - total[NQ:, LANES:]
            )
            sfield[it, h, 0, pl.ds(FL + f, NQ, stride=MSG), :] = (
                total[:NQ, LANES:] + total[NQ:, :LANES]
            )
            return carry

        lax.fori_loop(0, FL, one, 0, unroll=2)
        to_windows(it, h, 0)

    def transform(values):
        high, low = split(values)
        return dot(th[...], high) + (dot(tl[...], high) + dot(th[...], low))

    def window(it, h, k):
        traces_wait(rtraces, it, h, k, a2a_recv)
        received = rtraces[it, h, k // 2].reshape(NFD, 2, FL, LANES)
        spectra = jnp.concatenate(
            [received[:, 0].reshape(NF, LANES), received[:, 1].reshape(NF, LANES)], axis=1
        )
        times = transform(spectra)
        sample = lax.broadcasted_iota(jnp.int32, (NF, LANES), 0)
        nearest = jnp.minimum(sample, NF - sample)
        row = h % 2
        kept = jnp.where(nearest < onsets[row : row + 1, :], 1.0 / NF, 0.0).astype(F32)
        real = (times[:NF, :LANES] - times[NF:, LANES:]) * kept
        imag = (times[NF:, :LANES] + times[:NF, LANES:]) * kept
        back = transform(jnp.concatenate([real, imag], axis=1))
        back_real = back[:NF, :LANES] + back[NF:, LANES:]
        back_imag = back[:NF, LANES:] - back[NF:, :LANES]
        straces[it, h, k // 2] = jnp.concatenate(
            [back_real.reshape(NFD, 1, FL, LANES), back_imag.reshape(NFD, 1, FL, LANES)], axis=1
        ).reshape(TRACES, LANES)
        from_windows(it, h, k + 1)

    def windowed(it, h, k):
        if NW == 1:
            window(it, h, k)
        else:
            pl.when(lane == h // 2)(lambda: window(it, h, k))

    def rs_msg(source, target, it, h, number, dev):
        remote(source, target, rs_send.at[it, h], rs_recv.at[it, h, number], dev)

    def rs_second(it, h, row, direction, half):
        column, dev = ((yp, dev_p), (ym, dev_m))[direction]
        rs_msg(
            part.at[it, h, row * NY + column, rows_of(half)],
            r2.at[it, h, row * 2 + direction, rows_of(half)],
            it, h, 4 + row * 4 + direction * 2 + half, dev,
        )

    def adjoint(it, h):
        field_wait(rfield, it, h, 1, a2a_recv)

        def one(f, carry):
            real = rfield[it, h, 0, pl.ds(f, NQ, stride=MSG), :]
            imag = rfield[it, h, 0, pl.ds(FL + f, NQ, stride=MSG), :]
            field = jnp.concatenate(
                [
                    jnp.concatenate([real, imag], axis=1),
                    jnp.concatenate([imag, -real], axis=1),
                ],
                axis=0,
            )
            high, low = split(field)
            both = dot(jnp.concatenate([high, low], axis=0), rhi[f])
            total = both[: 2 * NQ] + both[2 * NQ :] + dot(high, rlo[f])
            rows = pl.ds(pl.multiple_of(f * FROWS, FROWS), FROWS)
            for s in range(NSD):
                part[it, h, s, rows, :] = total[:, s * LANES : (s + 1) * LANES]
            return carry

        lax.fori_loop(0, FL, one, 0, unroll=2)
        if it == ITERS - 1:
            write_upgoing(h)
        for row in range(2):
            for half, dev in ((0, dev_p), (1, dev_m)):
                rs_msg(
                    part.at[it, h, row * NY + y2, rows_of(half)],
                    r1.at[it, h, row * 2 + half],
                    it, h, row * 2 + half, dev,
                )
        for row in range(2):
            rs_second(it, h, row, 0, 1)
            rs_second(it, h, row, 1, 0)

    def rs_middle(it, h):
        for row in range(2):
            for half, column in ((0, yp), (1, ym)):
                landed(r1.at[it, h, row * 2 + half], rs_recv.at[it, h, row * 2 + half])
                slot = row * NY + column
                part[it, h, slot, rows_of(half), :] += r1[it, h, row * 2 + half]
                rs_second(it, h, row, half, half)

    def rs_column(it, h, row, half):
        for direction in range(2):
            landed(
                r2.at[it, h, row * 2 + direction, rows_of(half)],
                rs_recv.at[it, h, 4 + row * 4 + direction * 2 + half],
            )
        slot = row * NY + y
        part[it, h, slot, rows_of(half), :] += (
            r2[it, h, row * 2, rows_of(half), :] + r2[it, h, row * 2 + 1, rows_of(half), :]
        )

    def rs_columns(it, h):
        for half in range(2):
            rs_column(it, h, z1, half)
            rs_msg(
                part.at[it, h, z1 * NY + y, rows_of(half)],
                rz.at[it, h, rows_of(half)],
                it, h, 12 + half, dev_z,
            )
        for half in range(2):
            rs_column(it, h, z, half)

    def rs_finish(it, h):
        for half in range(2):
            landed(rz.at[it, h, rows_of(half)], rs_recv.at[it, h, 12 + half])
            for f in range(half * FL // 2, (half + 1) * FL // 2):
                for c in range(2):
                    rows = slice(f * FROWS + c * NQ, f * FROWS + (c + 1) * NQ)
                    sfield[it, h, 1, pl.ds(c * FL + f, NQ, stride=MSG), :] = (
                        part[it, h, src, rows, :] + rz[it, h, rows, :]
                    )
        to_windows(it, h, 2)

    def update(it, h):
        field_wait(rfield, it, h, 3, a2a_recv)
        for c in range(2):
            for f in range(FL):
                rows = slice(f * FROWS + c * NQ, f * FROWS + (c + 1) * NQ)
                field = rfield[it, h, 1, pl.ds(c * FL + f, NQ, stride=MSG), :]
                if it + 1 < ITERS:
                    ag[it + 1, h, src, rows, :] = ag[0, h, src, rows, :] - field
                else:
                    out[0, c, f, pl.ds(h, NQ, stride=NC), :] = field
        if it + 1 < ITERS:
            ag_start(it + 1, h)

    def write_upgoing(h):
        for c in range(2):
            for f in range(FL):
                out[1, c, f, pl.ds(h, NQ, stride=NC), :] = rfield[
                    ITERS - 1, h, 0, pl.ds(c * FL + f, NQ, stride=MSG), :
                ]

    steps = {
        "agz": ag_forward_z,
        "agy": ag_forward_y,
        "agf": ag_finish,
        "fwd": forward,
        "win": lambda it, h: windowed(it, h, 0),
        "adj": adjoint,
        "rsm": rs_middle,
        "rsc": rs_columns,
        "rsf": rs_finish,
        "win2": lambda it, h: windowed(it, h, 2),
        "upd": update,
    }

    lay_out(0)
    pl.semaphore_wait(barrier, len(greeted))
    signal_round(0, along_x)
    prepared = 0
    for step in ORDER:
        if step == "prep":
            prepare(prepared)
            prepared += 1
            if prepared == 2:
                pl.semaphore_wait(entered.at[0], 3)
                signal_round(1, along_z)
            if prepared == FL:
                pl.semaphore_wait(entered.at[1], 3)
            continue
        name, it, h = step.split()
        it, h = int(it), int(h)
        if name == "ags":
            if h > 0:
                lay_out(h)
            ag_start(it, h)
        else:
            steps[name](it, h)

    for it in range(ITERS):
        for h in range(NC):
            landed(ag.at[it, h, pl.ds(0, NSD - 1)], ag_send.at[it, h])
            landed(part.at[it, h, pl.ds(0, NSD - 1)], rs_send.at[it, h])
            for k in (0, 2):
                field_wait(sfield, it, h, k, a2a_send)
            for k in (1, 3):
                if NW == 1:
                    traces_wait(straces, it, h, k, a2a_send)
                else:
                    pl.when(lane == h // 2)(
                        lambda it=it, h=h, k=k: traces_wait(straces, it, h, k, a2a_send)
                    )


def per_device(reflection, focusing, onsets):
    high, low = tables()
    vmem = pl.BlockSpec(memory_space=pltpu.VMEM)
    fields = pl.pallas_call(
        kernel,
        out_shape=jax.ShapeDtypeStruct((2, *focusing.shape), F32),
        in_specs=[pl.BlockSpec(memory_space=pl.ANY), vmem, vmem, vmem, vmem],
        out_specs=vmem,
        scratch_shapes=[
            pltpu.VMEM((2, 2, LANES, 1024), F32),
            pltpu.VMEM((FL, 2 * LANES, 1024), BF16),
            pltpu.VMEM((FL, 2 * LANES, 1024), BF16),
            pltpu.VMEM((FL, 1024, 2 * LANES), BF16),
            pltpu.VMEM((FL, 1024, 2 * LANES), BF16),
            pltpu.VMEM((ITERS, NC, NSD, ROWS, LANES), F32),
            pltpu.VMEM((ITERS, NC, NSD, ROWS, LANES), F32),
            pltpu.VMEM((ITERS, NC, 4, HALF, LANES), F32),
            pltpu.VMEM((ITERS, NC, 4, ROWS, LANES), F32),
            pltpu.VMEM((ITERS, NC, ROWS, LANES), F32),
            pltpu.VMEM((ITERS, NC, 2, ROWS, LANES), F32),
            pltpu.VMEM((ITERS, NC, 2, ROWS, LANES), F32),
            pltpu.VMEM((ITERS, NC, 2, TRACES, LANES), F32),
            pltpu.VMEM((ITERS, NC, 2, TRACES, LANES), F32),
            pltpu.SemaphoreType.DMA((2,)),
            pltpu.SemaphoreType.DMA((ITERS, NC, 4)),
            pltpu.SemaphoreType.DMA((ITERS, NC, 4)),
            pltpu.SemaphoreType.DMA((ITERS, NC)),
            pltpu.SemaphoreType.DMA((ITERS, NC, 14)),
            pltpu.SemaphoreType.DMA((ITERS, NC)),
            pltpu.SemaphoreType.DMA((ITERS, NC, 14)),
            pltpu.SemaphoreType.REGULAR((2,)),
        ],
        compiler_params=pltpu.CompilerParams(
            collective_id=0, has_side_effects=True, vmem_limit_bytes=62 * 1024 * 1024
        ),
        name="marchenko",
    )(reflection, focusing, onsets, jnp.asarray(high), jnp.asarray(low))
    return focusing - fields[0], fields[1]


def solution(mesh):
    placed = (P(None, "freq", "src", None), P(None, "freq", None, "src"), P("freq", "src"))
    return jax.shard_map(
        per_device,
        mesh=mesh,
        in_specs=placed,
        out_specs=(P(None, "freq", None, "src"), P(None, "freq", None, "src")),
        check_vma=False,
    )
```
